256 devices in a mesh: dp: 8 (over y_hi, x), tp: 32 (over z, y_lo, core).
Axes of the slice: x: 4, y: 4 (y_hi: 2, y_lo: 2; y = y_hi * 2 + y_lo), z: 8, core: 2. Of those that a mesh axis runs over, the one named last changes fastest.
Arguments:
- tokens: bfloat16 [4096, 4096], P(('dp', 'tp')), may hold values from -6 to 6
- norm_scale_vector: float32 [4096], replicated, may hold values from 0.5 to 1.5
- gate_weight: bfloat16 [4096, 14336], P(None, 'tp'), may hold values from -0.09375 to 0.09375
- up_weight: bfloat16 [4096, 14336], P(None, 'tp'), may hold values from -0.09375 to 0.09375
- down_weight: bfloat16 [14336, 4096], P('tp'), may hold values from -0.046875 to 0.046875
- cotangent: bfloat16 [4096, 4096], P(('dp', 'tp')), may hold values from -4 to 4
Outputs:
- mixed: bfloat16 [4096, 4096], P(('dp', 'tp'))
- token_gradient: bfloat16 [4096, 4096], P(('dp', 'tp'))
- grad_gate: bfloat16 [4096, 14336], P('dp', 'tp')
- grad_up: bfloat16 [4096, 14336], P('dp', 'tp')
- grad_down: bfloat16 [14336, 4096], P('tp', 'dp')
The draws below stay inside these ranges and needn't reach their ends.
All inputs are finite; a program needn't handle non-finite values.
Results may differ from the reference program's by a relative error of at most 0.025.
Values may be sent and summed in bfloat16 or wider, within the bound.
A program may use at most 128 MiB of HBM per device.

```python
import jax
import jax.numpy as jnp
from jax import lax

D = 4096
FF = 14336
TOKENS = 4096
N_DP = 8
N_TP = 32


def shard_levels(rng, extent, cuts, low, top_value):
    def one(axis_at, shards_of):
        steps = jax.random.uniform(jax.random.fold_in(jax.random.fold_in(rng, 6), axis_at), (shards_of,), jnp.float32, low / len(cuts), top_value / len(cuts))
        return jnp.repeat(jnp.exp(steps), extent[axis_at] // shards_of).reshape((-1,) + (1,) * (len(extent) - axis_at - 1))

    loudness = one(*cuts[0])
    for cut in cuts[1:]:
        loudness = loudness * one(*cut)
    return loudness


def scatter_about(key, extent, deviation, bound, cuts=(), kind=jnp.bfloat16):
    entries = jax.random.normal(key, extent, jnp.float32) * deviation
    if len(cuts) > 0:
        entries = shard_levels(key, extent, cuts, -0.22, 0.18) * entries
    return jnp.clip(entries, min=-bound, max=bound).astype(kind)


def setup_inputs(seed: int = 0) -> dict:
    keys = jax.random.split(jax.random.key(seed), 7)
    return {
        "tokens": scatter_about(keys[0], (TOKENS, D), 1.0, 6.0, ((0, 256),)),
        "norm_scale_vector": jnp.clip(1.0 + 0.1 * jax.random.normal(keys[1], (D,), jnp.float32), 0.5, 1.5),
        "gate_weight": scatter_about(keys[2], (D, FF), D ** -0.5, 0.09375, ((1, 32),)),
        "up_weight": scatter_about(keys[3], (D, FF), D ** -0.5, 0.09375, ((1, 32),)),
        "down_weight": scatter_about(keys[4], (FF, D), FF ** -0.5, 0.046875, ((0, 32),)),
        "cotangent": scatter_about(keys[5], (TOKENS, D), 0.25, 4.0, ((0, 256),)),
    }


def replica_sum(left, right):
    rows = left.shape[0] // N_DP
    first = left.astype(jnp.float32).reshape(N_DP, rows, left.shape[1])
    second = right.astype(jnp.float32).reshape(N_DP, rows, right.shape[1])
    parts = jnp.einsum('nra,nrb->nab', first, second).astype(jnp.bfloat16)
    parts = lax.optimization_barrier(parts)
    return lax.optimization_barrier(jnp.sum(parts.astype(jnp.float32), axis=0)).astype(jnp.bfloat16)

def reference(tokens, norm_scale_vector, gate_weight, up_weight, down_weight, cotangent):
    expanded_hidden = tokens.astype(jnp.float32)
    reciprocal_root_mean = lax.rsqrt(lax.optimization_barrier(jnp.mean(expanded_hidden * expanded_hidden, axis=-1, keepdims=True)) + 1e-05)
    unit_input = expanded_hidden * reciprocal_root_mean
    rescaled_input = (unit_input * norm_scale_vector).astype(jnp.bfloat16)
    width = FF // N_TP

    def block(carry, index):
        first = (index * width).astype(jnp.int32)
        gate_block = lax.dynamic_slice_in_dim(gate_weight, first, width, 1)
        up_block = lax.dynamic_slice_in_dim(up_weight, first, width, 1)
        down_block = lax.dynamic_slice_in_dim(down_weight, first, width, 0)
        gate = jnp.dot(rescaled_input, gate_block, preferred_element_type=jnp.float32)
        lifted = jnp.dot(rescaled_input, up_block, preferred_element_type=jnp.float32)
        sigmoid_gate = jax.nn.sigmoid(gate)
        activated = gate * sigmoid_gate
        hidden = (activated * lifted).astype(jnp.bfloat16)
        partial_out = jnp.dot(hidden, down_block, preferred_element_type=jnp.float32).astype(jnp.bfloat16)
        grad_hidden = jnp.dot(cotangent, down_block.T, preferred_element_type=jnp.float32)
        grad_pre = (grad_hidden * lifted * sigmoid_gate * (1.0 + gate * (1.0 - sigmoid_gate))).astype(jnp.bfloat16)
        grad_lifted = (grad_hidden * activated).astype(jnp.bfloat16)
        partial_in = (jnp.dot(grad_pre, gate_block.T, preferred_element_type=jnp.float32) + jnp.dot(grad_lifted, up_block.T, preferred_element_type=jnp.float32)).astype(jnp.bfloat16)
        weight_gate = replica_sum(rescaled_input, grad_pre)
        weight_up = replica_sum(rescaled_input, grad_lifted)
        weight_down = replica_sum(hidden, cotangent)
        branch_sum, input_sum = carry
        carry = (branch_sum + partial_out.astype(jnp.float32), input_sum + partial_in.astype(jnp.float32))
        return (carry, (weight_gate, weight_up, weight_down))
    start = (jnp.zeros(tokens.shape, jnp.float32), jnp.zeros(tokens.shape, jnp.float32))
    (branch, grad_normed), (stack_gate, stack_up, stack_down) = lax.scan(block, start, jnp.arange(N_TP, dtype=jnp.int32))
    mixed = (expanded_hidden + branch).astype(jnp.bfloat16)
    gain_applied = grad_normed * norm_scale_vector
    inner_product = lax.optimization_barrier(jnp.mean(gain_applied * unit_input, axis=-1, keepdims=True))
    token_gradient = (cotangent.astype(jnp.float32) + reciprocal_root_mean * (gain_applied - unit_input * inner_product)).astype(jnp.bfloat16)
    grad_gate = jnp.transpose(stack_gate, (1, 0, 2)).reshape(D, FF)
    grad_up = jnp.transpose(stack_up, (1, 0, 2)).reshape(D, FF)
    grad_down = stack_down.reshape(FF, D)
    return (mixed, token_gradient, grad_gate, grad_up, grad_down)
```

```python
import functools

import jax
import jax.numpy as jnp
from jax import lax
from jax.experimental import pallas as pl
from jax.experimental.pallas import tpu as pltpu
from jax.sharding import PartitionSpec as P

BF16 = jnp.bfloat16
F32 = jnp.float32
MESH = pl.DeviceIdType.MESH
D = 4096
W = 448
ROWS = 16
NZ = 8
SPLIT = 2048
HALF = 2048
CH = 512
TILE = 512


def kernel(
    tok, scale, cot, gw, uw, dw,
    mixed, tgrad, wout,
    nrm, ctg, ext, wg, wu, wd, acc, hid, gpr, glf, tra, part, crecv, zrecv, yst, yrecv,
    wch, xr1, xr2, lsem, ssem, rsem,
):
    d, t = lax.axis_index("dp"), lax.axis_index("tp")
    yh, x = d // 4, d % 4
    z, yl, c = t // 4, (t // 2) % 2, t % 2
    zdev = {s: (d, ((z + s + NZ) % NZ) * 4 + yl * 2 + c) for s in (1, -1)}
    ydev = (d, z * 4 + (1 - yl) * 2 + c)
    cdev = (d, z * 4 + yl * 2 + (1 - c))
    xdev = {s: (yh * 4 + (x + s + 4) % 4, t) for s in (1, -1)}
    hdev = ((1 - yh) * 4 + x, t)
    partners = [zdev[1], zdev[-1], ydev, cdev, xdev[1], xdev[-1], hdev]

    loads = [
        pltpu.make_async_copy(src, dst, lsem.at[i])
        for i, (src, dst) in enumerate(((gw, wg), (uw, wu), (dw, wd)))
    ]
    for load in loads:
        load.start()

    sent = []

    def send(src, dst, device):
        at = len(sent)
        copy = pltpu.make_async_remote_copy(
            src_ref=src, dst_ref=dst, send_sem=ssem.at[at], recv_sem=rsem.at[at],
            device_id=device, device_id_type=MESH,
        )
        copy.start()
        sent.append(copy)
        return copy

    def normalized():
        xf = tok[...].astype(F32)
        r = lax.rsqrt(jnp.mean(xf * xf, axis=-1, keepdims=True) + 1e-05)
        return xf, r, xf * r

    nrm[z, yl, c] = (normalized()[2] * scale[...]).astype(BF16)
    ctg[z, yl, c] = cot[...]

    barrier = pltpu.get_barrier_semaphore()
    for device in partners:
        pl.semaphore_signal(barrier, inc=1, device_id=device, device_id_type=MESH)
    pl.semaphore_wait(barrier, len(partners))

    def gather(buf):
        def cols(lo, hi, h, s):
            if h < 4:
                return pl.ds(lo, hi - lo)
            mid = (lo + hi) // 2
            return pl.ds(lo, mid - lo) if s == 1 else pl.ds(mid, hi - mid)

        def a_slab(zz, h, s):
            return buf.at[zz, yl, c, :, cols(0, SPLIT, h, s)]

        def b_slab(zz, h, s):
            return buf.at[zz, pl.ds(0, 2), c, :, cols(SPLIT, D, h, s)]

        own_b = buf.at[z, yl, c, :, pl.ds(SPLIT, D - SPLIT)]
        yb = send(own_b, own_b, ydev)
        za, zb = {}, {}
        for s in (1, -1):
            za[s] = send(a_slab(z, 1, s), a_slab(z, 1, s), zdev[s])
        ya = send(a_slab(z, 1, 1), a_slab(z, 1, 1), ydev)
        yield
        yb.wait_recv()
        for s in (1, -1):
            zb[s] = send(b_slab(z, 1, s), b_slab(z, 1, s), zdev[s])
        yield
        pending, core = [(z, [ya])], []

        def flush():
            for zz, arrivals in pending:
                for arrival in arrivals:
                    arrival.wait_recv()
                both = buf.at[zz, pl.ds(0, 2), c]
                core.append(send(both, both, cdev))

        for h in (1, 2, 3, 4):
            fresh = []
            for s in (1, -1):
                zz = (z - s * h + NZ) % NZ
                za[s].wait_recv()
                if h < 4:
                    za[s] = send(a_slab(zz, h + 1, s), a_slab(zz, h + 1, s), zdev[s])
                yf = send(a_slab(zz, h, s), a_slab(zz, h, s), ydev)
                zb[s].wait_recv()
                if h < 4:
                    zb[s] = send(b_slab(zz, h + 1, s), b_slab(zz, h + 1, s), zdev[s])
                if h == 4 and s == -1:
                    fresh[0][1].append(yf)
                else:
                    fresh.append((zz, [yf]))
            yield
            flush()
            pending = fresh
            yield
        flush()
        for copy in core:
            copy.wait_recv()

    def run(*gens):
        live = list(gens)
        while live:
            for g in list(live):
                if next(g, 1) == 1:
                    live.remove(g)

    half = pl.ds(pl.multiple_of((1 - yh) * HALF, HALF), HALF)
    seeds = [
        send(src.at[z, yl, c, :, half], ext.at[z, yl, c, :, pl.ds(i * HALF, HALF)], hdev)
        for i, src in enumerate((nrm, ctg))
    ]
    run(gather(nrm), gather(ctg))

    def seeded():
        for seed in seeds:
            seed.wait_recv()
        yield from gather(ext)

    third = seeded()

    def tokens_of(buf, col, width):
        return buf[:, :, :, :, pl.ds(col, width)].reshape(NZ * 4 * ROWS, width)

    for load in loads:
        load.wait()

    next(third, None)
    acc[...] = jnp.zeros_like(acc)

    def into(i, buf, weight):
        @pl.loop(0, D // TILE)
        def _(k):
            at = pl.multiple_of(k * TILE, TILE)
            acc[i] += jnp.dot(
                tokens_of(buf, at, TILE), weight[pl.ds(at, TILE), :],
                preferred_element_type=F32,
            )

    into(0, nrm, wg)
    next(third, None)
    into(1, nrm, wu)
    next(third, None)

    @pl.loop(0, D // TILE)
    def _(k):
        at = pl.multiple_of(k * TILE, TILE)
        acc[2] += lax.dot_general(
            tokens_of(ctg, at, TILE), wd[:, pl.ds(at, TILE)], (((1,), (1,)), ((), ())),
            preferred_element_type=F32,
        )

    next(third, None)

    @pl.loop(0, 4)
    def _(k):
        rows = pl.ds(pl.multiple_of(k * 128, 128), 128)
        gate, lifted, gh = acc[0, rows, :], acc[1, rows, :], acc[2, rows, :]
        sg = jax.nn.sigmoid(gate)
        act = gate * sg
        h = act * lifted
        gp = gh * lifted * sg * (1.0 + gate * (1.0 - sg))
        gl = gh * act
        hid[rows, :] = h.astype(BF16)
        gpr[rows, :] = gp.astype(BF16)
        glf[rows, :] = gl.astype(BF16)
        tra[0, pl.ds(0, W), rows] = h.T.astype(BF16)
        tra[0, pl.ds(W, W), rows] = gp.T.astype(BF16)
        tra[0, pl.ds(2 * W, W), rows] = gl.T.astype(BF16)

    swaps = []
    for g in range(3):
        rows = pl.ds(g * W, W)
        swaps.append(send(tra.at[0, rows], tra.at[1, rows], hdev))

    next(third, None)

    @pl.loop(0, D // TILE)
    def _(k):
        at = pl.multiple_of(k * TILE, TILE)
        out = jnp.dot(hid[...], wd[:, pl.ds(at, TILE)], preferred_element_type=F32)
        part[0, :, :, :, :, pl.ds(at, TILE)] = out.astype(BF16).reshape(NZ, 2, 2, ROWS, TILE)

    def scatter(i):
        theirs = part.at[i, pl.ds(0, NZ), pl.ds(0, 2), 1 - c]
        core = send(theirs, crecv.at[i], cdev)
        yield
        core.wait_recv()
        arrived = {}
        for h in range(4):
            for s in (1, -1):
                zz = (z + s * (4 - h) + NZ) % NZ
                if h == 0:
                    cols = pl.ds(0, D // 2) if s == 1 else pl.ds(D // 2, D // 2)
                    total = part[i, zz, :, c, :, cols].astype(F32) + crecv[i, zz, :, :, cols].astype(F32)
                    part[i, zz, :, c, :, cols] = total.astype(BF16)
                else:
                    arrived[s].wait_recv()
                    for cols, added in (
                        (pl.ds(0, D // 2), h > 1 or s == 1),
                        (pl.ds(D // 2, D // 2), h > 1 or s == -1),
                    ):
                        total = part[i, zz, :, c, :, cols].astype(F32) + crecv[i, zz, :, :, cols].astype(F32)
                        if added:
                            total = total + zrecv[i, s2(s), h - 1, :, :, cols].astype(F32)
                        part[i, zz, :, c, :, cols] = total.astype(BF16)
                    cols = pl.ds(0, D)
                arrived[s] = send(
                    part.at[i, zz, pl.ds(0, 2), c, :, cols],
                    zrecv.at[i, s2(s), h, pl.ds(0, 2), :, cols],
                    zdev[s],
                )
            yield
        for s in (1, -1):
            arrived[s].wait_recv()

        def total_of(y):
            return (
                part[i, z, y, c].astype(F32) + crecv[i, z, y].astype(F32)
                + zrecv[i, 0, 3, y].astype(F32) + zrecv[i, 1, 3, y].astype(F32)
            )

        yst[i] = total_of(1 - yl).astype(BF16)
        last = send(yst.at[i], yrecv.at[i], ydev)
        yield
        last.wait_recv()
        total = total_of(yl) + yrecv[i].astype(F32)
        xf, r, unit = normalized()
        if i == 0:
            mixed[...] = (xf + total).astype(BF16)
        else:
            gain = total * scale[...]
            inner = jnp.mean(gain * unit, axis=-1, keepdims=True)
            tgrad[...] = (cot[...].astype(F32) + r * (gain - unit * inner)).astype(BF16)

    def s2(s):
        return 0 if s == 1 else 1

    forward = scatter(0)
    next(forward)
    next(third, None)

    @pl.loop(0, D // TILE)
    def _(k):
        at = pl.multiple_of(k * TILE, TILE)
        dims = (((1,), (1,)), ((), ()))
        out = lax.dot_general(gpr[...], wg[pl.ds(at, TILE), :], dims, preferred_element_type=F32)
        out += lax.dot_general(glf[...], wu[pl.ds(at, TILE), :], dims, preferred_element_type=F32)
        part[1, :, :, :, :, pl.ds(at, TILE)] = out.astype(BF16).reshape(NZ, 2, 2, ROWS, TILE)

    backward = scatter(1)
    next(backward)
    next(forward)
    run(third)
    next(backward)

    q = W // 2

    def weights(g, xx):
        rows = pl.ds(g * W, W)
        own = ctg if g == 0 else nrm
        at = pl.multiple_of(yh * HALF + xx * CH, CH)
        far = pl.multiple_of((HALF if g == 0 else 0) + xx * CH, CH)
        out = jnp.dot(tra[0, rows, :], tokens_of(own, at, CH), preferred_element_type=F32)
        out += jnp.dot(tra[1, rows, :], tokens_of(ext, far, CH), preferred_element_type=F32)
        return out

    def over_x(g):
        up, down = pl.ds(g * W, q), pl.ds(g * W + q, q)
        rows = pl.ds(g * W, W)
        swaps[g].wait_recv()
        far = (x + 2) % 4
        wch[0, rows, :] = weights(g, far).astype(BF16)
        one = send(wch.at[0, up], xr1.at[0, pl.ds(g * q, q)], xdev[1])
        two = send(wch.at[0, down], xr1.at[1, pl.ds(g * q, q)], xdev[-1])
        wch[1, rows, :] = weights(g, (x + 1) % 4).astype(BF16)
        three = send(wch.at[1, down], xr2.at[0, down], xdev[1])
        wch[2, rows, :] = weights(g, (x + 3) % 4).astype(BF16)
        four = send(wch.at[2, up], xr2.at[1, up], xdev[-1])
        yield
        one.wait_recv()
        wch[1, up, :] = (wch[1, up, :].astype(F32) + xr1[0, pl.ds(g * q, q)].astype(F32)).astype(BF16)
        five = send(wch.at[1, up], xr2.at[0, up], xdev[1])
        two.wait_recv()
        wch[2, down, :] = (wch[2, down, :].astype(F32) + xr1[1, pl.ds(g * q, q)].astype(F32)).astype(BF16)
        six = send(wch.at[2, down], xr2.at[1, down], xdev[-1])
        yield
        mine = weights(g, x)
        for copy in (three, four, five, six):
            copy.wait_recv()
        wout[rows, :] = (mine + xr2[0, rows].astype(F32) + xr2[1, rows].astype(F32)).astype(BF16)

    thirds = [over_x(g) for g in range(3)]
    next(thirds[0])
    next(forward)
    next(backward)
    next(thirds[0])
    next(thirds[1])
    next(forward)
    next(backward)
    next(thirds[1])
    next(thirds[2])
    next(forward)
    next(backward)
    run(thirds[0])
    next(thirds[2])
    next(forward)
    next(backward)
    run(thirds[1])
    run(forward)
    run(backward)
    run(thirds[2])

    for copy in sent:
        copy.wait_send()


def local(tokens, norm_scale_vector, gate_weight, up_weight, down_weight, cotangent):
    vmem = pl.BlockSpec(memory_space=pltpu.VMEM)
    hbm = pl.BlockSpec(memory_space=pl.ANY)
    slab = (NZ, 2, 2, ROWS, D)
    count = 192
    mixed, tgrad, wout = pl.pallas_call(
        kernel,
        out_shape=(
            jax.ShapeDtypeStruct((ROWS, D), BF16),
            jax.ShapeDtypeStruct((ROWS, D), BF16),
            jax.ShapeDtypeStruct((3 * W, CH), BF16),
        ),
        in_specs=[vmem, vmem, vmem, hbm, hbm, hbm],
        out_specs=(vmem, vmem, vmem),
        scratch_shapes=[
            pltpu.VMEM(slab, BF16),
            pltpu.VMEM(slab, BF16),
            pltpu.VMEM(slab, BF16),
            pltpu.VMEM((D, W), BF16),
            pltpu.VMEM((D, W), BF16),
            pltpu.VMEM((W, D), BF16),
            pltpu.VMEM((3, 512, W), F32),
            pltpu.VMEM((512, W), BF16),
            pltpu.VMEM((512, W), BF16),
            pltpu.VMEM((512, W), BF16),
            pltpu.VMEM((2, 3 * W, 512), BF16),
            pltpu.VMEM((2, *slab), BF16),
            pltpu.VMEM((2, NZ, 2, ROWS, D), BF16),
            pltpu.VMEM((2, 2, 4, 2, ROWS, D), BF16),
            pltpu.VMEM((2, ROWS, D), BF16),
            pltpu.VMEM((2, ROWS, D), BF16),
            pltpu.VMEM((3, 3 * W, CH), BF16),
            pltpu.VMEM((2, 3 * W // 2, CH), BF16),
            pltpu.VMEM((2, 3 * W, CH), BF16),
            pltpu.SemaphoreType.DMA((3,)),
            pltpu.SemaphoreType.DMA((count,)),
            pltpu.SemaphoreType.DMA((count,)),
        ],
        compiler_params=pltpu.CompilerParams(
            collective_id=0, has_side_effects=True, vmem_limit_bytes=62 << 20
        ),
        cost_estimate=pl.CostEstimate(
            flops=2 * 9 * 512 * D * W, bytes_accessed=16 << 20, transcendentals=512 * W
        ),
        name="ffn",
    )(tokens, norm_scale_vector.reshape(1, D), cotangent, gate_weight, up_weight, down_weight)
    return mixed, tgrad, wout[W : 2 * W].T, wout[2 * W :].T, wout[:W]


def solution(mesh):
    both, rows = P(("dp", "tp"), None), P()
    return jax.shard_map(
        local,
        mesh=mesh,
        in_specs=(both, rows, P(None, "tp"), P(None, "tp"), P("tp", None), both),
        out_specs=(both, both, P("dp", "tp"), P("dp", "tp"), P("tp", "dp")),
        check_vma=False,
    )
```

```python
import functools

import jax
import jax.numpy as jnp
from jax import lax
from jax.experimental import pallas as pl
from jax.experimental.pallas import tpu as pltpu
from jax.sharding import PartitionSpec as P

BF16 = jnp.bfloat16
F32 = jnp.float32
MESH = pl.DeviceIdType.MESH
D = 4096
W = 448
ROWS = 16
NZ = 8
HALF = 2048
CH = 512
TILE = 512


def kernel(
    tok, scale, cot, gw, uw, dw,
    mixed, tgrad, wout,
    nrm, ctg, ext, wg, wu, wd, acc, hid, gpr, glf, tra, got, part, crecv, zrecv, yst, yrecv,
    vch, vr1, vr2, vst, vrecv, wch, xr1, xr2, lsem, ssem, rsem,
):
    d, t = lax.axis_index("dp"), lax.axis_index("tp")
    yh, x = d // 4, d % 4
    z, yl, c = t // 4, (t // 2) % 2, t % 2
    zdev = {s: (d, ((z + s + NZ) % NZ) * 4 + yl * 2 + c) for s in (1, -1)}
    ydev = (d, z * 4 + (1 - yl) * 2 + c)
    cdev = (d, z * 4 + yl * 2 + (1 - c))
    xdev = {s: (yh * 4 + (x + s + 4) % 4, t) for s in (1, -1)}
    hdev = ((1 - yh) * 4 + x, t)
    partners = [zdev[1], zdev[-1], ydev, cdev, xdev[1], xdev[-1], hdev]

    barrier = pltpu.get_barrier_semaphore()
    for device in partners:
        pl.semaphore_signal(barrier, inc=1, device_id=device, device_id_type=MESH)

    loads = [
        pltpu.make_async_copy(src, dst, lsem.at[i])
        for i, (src, dst) in enumerate(((gw, wg), (uw, wu), (dw, wd)))
    ]
    for load in loads:
        load.start()

    sent = []

    def send(src, dst, device):
        at = len(sent)
        copy = pltpu.make_async_remote_copy(
            src_ref=src, dst_ref=dst, send_sem=ssem.at[at], recv_sem=rsem.at[at],
            device_id=device, device_id_type=MESH,
        )
        copy.start()
        sent.append(copy)
        return copy

    def normalized():
        xf = tok[...].astype(F32)
        r = lax.rsqrt(jnp.mean(xf * xf, axis=-1, keepdims=True) + 1e-05)
        return xf, r, xf * r

    nrm[z, yl, c] = (normalized()[2] * scale[...]).astype(BF16)
    ctg[z, yl, c] = cot[...]
    pl.semaphore_wait(barrier, len(partners))

    def gather(buf, width):
        def one(zz, y, s=0):
            mid = width // 2
            cols = {0: pl.ds(0, width), 1: pl.ds(0, mid), -1: pl.ds(mid, mid)}[s]
            return buf.at[zz, y, c, :, cols]

        def both(zz, s=0):
            mid = width // 2
            cols = {0: pl.ds(0, width), 1: pl.ds(0, mid), -1: pl.ds(mid, mid)}[s]
            return buf.at[zz, pl.ds(0, 2), c, :, cols]

        def push(ref, device):
            return send(ref, ref, device)

        at = {(s, h): (z - s * h + NZ) % NZ for s in (1, -1) for h in (1, 2, 3, 4)}
        ways = (1, -1)
        z1 = {s: push(one(z, yl), zdev[s]) for s in ways}
        y0 = push(one(z, yl), ydev)
        yield
        z2, y1 = {}, {}
        for s in ways:
            z1[s].wait_recv()
            z2[s] = push(one(at[s, 1], yl), zdev[s])
            y1[s] = push(one(at[s, 1], yl), ydev)
        yield
        y0.wait_recv()
        core = [push(both(z), cdev)]
        z3, y2, z3b = {}, {}, {}
        for s in ways:
            z2[s].wait_recv()
            z3[s] = push(one(at[s, 2], yl), zdev[s])
            y2[s] = push(one(at[s, 2], yl), ydev)
        yield
        for s in ways:
            y1[s].wait_recv()
            core.append(push(both(at[s, 1]), cdev))
        for s in ways:
            y2[s].wait_recv()
            z3b[s] = push(one(at[s, 2], 1 - yl), zdev[s])
        yield
        z4, z4b = {}, {}
        for s in ways:
            core.append(push(both(at[s, 2]), cdev))
        for s in ways:
            z3[s].wait_recv()
            z4[s] = push(one(at[s, 3], yl, s), zdev[s])
        yield
        for s in ways:
            z3b[s].wait_recv()
            z4b[s] = push(one(at[s, 3], 1 - yl, s), zdev[s])
            core.append(push(both(at[s, 3]), cdev))
        yield
        for s in ways:
            z4[s].wait_recv()
            z4b[s].wait_recv()
            core.append(push(both(at[s, 4], s), cdev))
        yield
        for copy in core:
            copy.wait_recv()

    def run(*gens):
        live = list(gens)
        while live:
            for g in list(live):
                if next(g, 1) == 1:
                    live.remove(g)

    half = pl.ds(pl.multiple_of((1 - yh) * HALF, HALF), HALF)
    normed, cots = gather(nrm, D), gather(ctg, D)
    next(normed)
    next(cots)
    seed = send(nrm.at[z, yl, c, :, half], ext.at[z, yl, c], hdev)

    def seeded():
        seed.wait_recv()
        yield from gather(ext, HALF)

    third = seeded()
    run(normed, cots)
    next(third)

    def tokens_of(buf, col, width):
        return buf[:, :, :, :, pl.ds(col, width)].reshape(NZ * 4 * ROWS, width)

    acc[...] = jnp.zeros_like(acc)

    def into(i, buf, weight):
        @pl.loop(0, D // TILE)
        def _(k):
            at = pl.multiple_of(k * TILE, TILE)
            acc[i] += lax.dot_general(
                tokens_of(buf, at, TILE), weight[:, pl.ds(at, TILE)], (((1,), (1,)), ((), ())),
                preferred_element_type=F32,
            )

    for load in loads:
        load.wait()
    into(0, nrm, wg)
    next(third)
    into(1, nrm, wu)
    next(third)

    @pl.loop(0, 4)
    def _(k):
        rows = pl.ds(pl.multiple_of(k * 128, 128), 128)
        gate, lifted = acc[0, rows, :], acc[1, rows, :]
        h = gate * jax.nn.sigmoid(gate) * lifted
        hid[rows, :] = h.astype(BF16)
        tra[pl.ds(0, W), rows] = h.T.astype(BF16)

    next(third)

    def down(other, xx):
        at = pl.multiple_of(other * HALF + xx * CH, CH)
        return jnp.dot(tra[pl.ds(0, W), :], tokens_of(ctg, at, CH), preferred_element_type=F32)

    def downs():
        far = (x + 2) % 4
        after, before = (x + 1) % 4, (x + 3) % 4
        vch[0] = down(0, far).astype(BF16)
        one = send(vch.at[0], vr1.at[0], xdev[1])
        vch[1] = down(1, far).astype(BF16)
        two = send(vch.at[1], vr1.at[1], xdev[-1])
        vch[2] = down(1, after).astype(BF16)
        three = send(vch.at[2], vr2.at[0, 1], xdev[1])
        vch[3] = down(0, before).astype(BF16)
        four = send(vch.at[3], vr2.at[1, 0], xdev[-1])
        yield
        vch[4] = down(0, after).astype(BF16)
        vch[5] = down(1, before).astype(BF16)
        yield
        one.wait_recv()
        vch[4] = (vch[4].astype(F32) + vr1[0].astype(F32)).astype(BF16)
        five = send(vch.at[4], vr2.at[0, 0], xdev[1])
        two.wait_recv()
        vch[5] = (vch[5].astype(F32) + vr1[1].astype(F32)).astype(BF16)
        six = send(vch.at[5], vr2.at[1, 1], xdev[-1])
        yield
        theirs, mine = down(1 - yh, x), down(yh, x)
        for copy in (three, four, five, six):
            copy.wait_recv()
        vst[...] = (theirs + vr2[0, 1 - yh].astype(F32) + vr2[1, 1 - yh].astype(F32)).astype(BF16)
        last = send(vst, vrecv, hdev)
        yield
        mine = mine + vr2[0, yh].astype(F32) + vr2[1, yh].astype(F32)
        last.wait_recv()
        wout[pl.ds(0, W), :] = (mine + vrecv[...].astype(F32)).astype(BF16)

    down_sum = downs()
    next(down_sum)
    next(third)

    @pl.loop(0, D // TILE)
    def _(k):
        at = pl.multiple_of(k * TILE, TILE)
        out = jnp.dot(hid[...], wd[:, pl.ds(at, TILE)], preferred_element_type=F32)
        part[0, :, :, :, :, pl.ds(at, TILE)] = out.astype(BF16).reshape(NZ, 2, 2, ROWS, TILE)

    def s2(s):
        return 0 if s == 1 else 1

    def scatter(i):
        theirs = part.at[i, pl.ds(0, NZ), pl.ds(0, 2), 1 - c]
        core = send(theirs, crecv.at[i], cdev)
        yield
        core.wait_recv()
        arrived = {}
        for h in range(4):
            for s in (1, -1):
                zz = (z + s * (4 - h) + NZ) % NZ
                if h == 0:
                    cols = pl.ds(0, D // 2) if s == 1 else pl.ds(D // 2, D // 2)
                    total = part[i, zz, :, c, :, cols].astype(F32) + crecv[i, zz, :, :, cols].astype(F32)
                    part[i, zz, :, c, :, cols] = total.astype(BF16)
                else:
                    arrived[s].wait_recv()
                    for cols, added in (
                        (pl.ds(0, D // 2), h > 1 or s == 1),
                        (pl.ds(D // 2, D // 2), h > 1 or s == -1),
                    ):
                        total = part[i, zz, :, c, :, cols].astype(F32) + crecv[i, zz, :, :, cols].astype(F32)
                        if added:
                            total = total + zrecv[i, s2(s), h - 1, :, :, cols].astype(F32)
                        part[i, zz, :, c, :, cols] = total.astype(BF16)
                    cols = pl.ds(0, D)
                arrived[s] = send(
                    part.at[i, zz, pl.ds(0, 2), c, :, cols],
                    zrecv.at[i, s2(s), h, pl.ds(0, 2), :, cols],
                    zdev[s],
                )
            yield
        for s in (1, -1):
            arrived[s].wait_recv()

        def total_of(y):
            return (
                part[i, z, y, c].astype(F32) + crecv[i, z, y].astype(F32)
                + zrecv[i, 0, 3, y].astype(F32) + zrecv[i, 1, 3, y].astype(F32)
            )

        yst[i] = total_of(1 - yl).astype(BF16)
        last = send(yst.at[i], yrecv.at[i], ydev)
        yield
        last.wait_recv()
        total = total_of(yl) + yrecv[i].astype(F32)
        xf, r, unit = normalized()
        if i == 0:
            mixed[...] = (xf + total).astype(BF16)
        else:
            gain = total * scale[...]
            inner = jnp.mean(gain * unit, axis=-1, keepdims=True)
            tgrad[...] = (cot[...].astype(F32) + r * (gain - unit * inner)).astype(BF16)

    forward = scatter(0)
    next(forward)
    next(third)
    into(2, ctg, wd)
    next(forward)
    next(third)

    @pl.loop(0, 4)
    def _(k):
        rows = pl.ds(pl.multiple_of(k * 128, 128), 128)
        gate, lifted, gh = acc[0, rows, :], acc[1, rows, :], acc[2, rows, :]
        sg = jax.nn.sigmoid(gate)
        gp = gh * lifted * sg * (1.0 + gate * (1.0 - sg))
        gl = gh * (gate * sg)
        gpr[rows, :] = gp.astype(BF16)
        glf[rows, :] = gl.astype(BF16)
        tra[pl.ds(W, W), rows] = gp.T.astype(BF16)
        tra[pl.ds(2 * W, W), rows] = gl.T.astype(BF16)

    swaps = []
    for g in range(2):
        rows = pl.ds((g + 1) * W, W)
        swaps.append(send(tra.at[rows], got.at[g], hdev))

    next(down_sum)

    @pl.loop(0, D // TILE)
    def _(k):
        at = pl.multiple_of(k * TILE, TILE)
        out = jnp.dot(gpr[...], wg[:, pl.ds(at, TILE)], preferred_element_type=F32)
        out += jnp.dot(glf[...], wu[:, pl.ds(at, TILE)], preferred_element_type=F32)
        part[1, :, :, :, :, pl.ds(at, TILE)] = out.astype(BF16).reshape(NZ, 2, 2, ROWS, TILE)

    backward = scatter(1)
    next(backward)
    run(third)
    next(forward)
    next(down_sum)
    next(backward)

    q = W // 2

    def weights(g, xx):
        at = pl.multiple_of(yh * HALF + xx * CH, CH)
        far = pl.multiple_of(xx * CH, CH)
        out = jnp.dot(tra[pl.ds((g + 1) * W, W), :], tokens_of(nrm, at, CH), preferred_element_type=F32)
        out += jnp.dot(got[g], tokens_of(ext, far, CH), preferred_element_type=F32)
        return out

    def over_x(g):
        up, down = pl.ds(0, q), pl.ds(q, q)
        swaps[g].wait_recv()
        far = (x + 2) % 4
        wch[g, 0] = weights(g, far).astype(BF16)
        one = send(wch.at[g, 0, up], xr1.at[g, 0], xdev[1])
        two = send(wch.at[g, 0, down], xr1.at[g, 1], xdev[-1])
        wch[g, 1] = weights(g, (x + 1) % 4).astype(BF16)
        three = send(wch.at[g, 1, down], xr2.at[g, 0, down], xdev[1])
        wch[g, 2] = weights(g, (x + 3) % 4).astype(BF16)
        four = send(wch.at[g, 2, up], xr2.at[g, 1, up], xdev[-1])
        yield
        one.wait_recv()
        wch[g, 1, up] = (wch[g, 1, up].astype(F32) + xr1[g, 0].astype(F32)).astype(BF16)
        five = send(wch.at[g, 1, up], xr2.at[g, 0, up], xdev[1])
        two.wait_recv()
        wch[g, 2, down] = (wch[g, 2, down].astype(F32) + xr1[g, 1].astype(F32)).astype(BF16)
        six = send(wch.at[g, 2, down], xr2.at[g, 1, down], xdev[-1])
        yield
        mine = weights(g, x)
        for copy in (three, four, five, six):
            copy.wait_recv()
        total = mine + xr2[g, 0].astype(F32) + xr2[g, 1].astype(F32)
        wout[pl.ds((g + 1) * W, W), :] = total.astype(BF16)

    gate_sum, up_sum = over_x(0), over_x(1)
    next(forward)
    next(backward)
    next(gate_sum)
    next(forward)
    next(backward)
    next(up_sum)
    next(down_sum)
    next(forward)
    next(backward)
    next(gate_sum)
    run(forward)
    next(backward)
    run(down_sum)
    next(up_sum)
    run(backward)
    run(gate_sum)
    run(up_sum)

    for copy in sent:
        copy.wait_send()


def finish(mixed, tgrad, wout, mixed_out, tgrad_out, gate_out, up_out, down_out):
    mixed_out[...] = mixed[...]
    tgrad_out[...] = tgrad[...]
    gate_out[...] = wout[W : 2 * W]
    up_out[...] = wout[2 * W :]
    down_out[...] = wout[:W]


def local(tokens, norm_scale_vector, gate_weight, up_weight, down_weight, cotangent):
    vmem = pl.BlockSpec(memory_space=pltpu.VMEM)
    hbm = pl.BlockSpec(memory_space=pl.ANY)
    slab = (NZ, 2, 2, ROWS, D)
    count = 128
    mixed, tgrad, wout = pl.pallas_call(
        kernel,
        out_shape=(
            jax.ShapeDtypeStruct((ROWS, D), BF16),
            jax.ShapeDtypeStruct((ROWS, D), BF16),
            jax.ShapeDtypeStruct((3 * W, CH), BF16),
        ),
        in_specs=[vmem, vmem, vmem, hbm, hbm, hbm],
        out_specs=(vmem, vmem, vmem),
        scratch_shapes=[
            pltpu.VMEM(slab, BF16),
            pltpu.VMEM(slab, BF16),
            pltpu.VMEM((NZ, 2, 2, ROWS, HALF), BF16),
            pltpu.VMEM((W, D), BF16),
            pltpu.VMEM((W, D), BF16),
            pltpu.VMEM((W, D), BF16),
            pltpu.VMEM((3, 512, W), F32),
            pltpu.VMEM((512, W), BF16),
            pltpu.VMEM((512, W), BF16),
            pltpu.VMEM((512, W), BF16),
            pltpu.VMEM((3 * W, 512), BF16),
            pltpu.VMEM((2, W, 512), BF16),
            pltpu.VMEM((2, *slab), BF16),
            pltpu.VMEM((2, NZ, 2, ROWS, D), BF16),
            pltpu.VMEM((2, 2, 4, 2, ROWS, D), BF16),
            pltpu.VMEM((2, ROWS, D), BF16),
            pltpu.VMEM((2, ROWS, D), BF16),
            pltpu.VMEM((6, W, CH), BF16),
            pltpu.VMEM((2, W, CH), BF16),
            pltpu.VMEM((2, 2, W, CH), BF16),
            pltpu.VMEM((W, CH), BF16),
            pltpu.VMEM((W, CH), BF16),
            pltpu.VMEM((2, 3, W, CH), BF16),
            pltpu.VMEM((2, 2, W // 2, CH), BF16),
            pltpu.VMEM((2, 2, W, CH), BF16),
            pltpu.SemaphoreType.DMA((3,)),
            pltpu.SemaphoreType.DMA((count,)),
            pltpu.SemaphoreType.DMA((count,)),
        ],
        compiler_params=pltpu.CompilerParams(
            collective_id=0, has_side_effects=True, vmem_limit_bytes=62 << 20
        ),
        cost_estimate=pl.CostEstimate(
            flops=2 * 9 * 512 * D * W, bytes_accessed=16 << 20, transcendentals=512 * W
        ),
        name="ffn",
    )(tokens, norm_scale_vector.reshape(1, D), cotangent, gate_weight.T, up_weight.T, down_weight)
    block = jax.ShapeDtypeStruct((W, CH), BF16)
    mixed, tgrad, gate, up, down = pl.pallas_call(
        finish,
        out_shape=(*(jax.ShapeDtypeStruct(v.shape, v.dtype) for v in (mixed, tgrad)), block, block, block),
        in_specs=[vmem] * 3,
        out_specs=(vmem,) * 5,
        compiler_params=pltpu.CompilerParams(vmem_limit_bytes=62 << 20),
        name="finish",
    )(mixed, tgrad, wout)
    return mixed, tgrad, gate.T, up.T, down


def solution(mesh):
    both, rows = P(("dp", "tp"), None), P()
    return jax.shard_map(
        local,
        mesh=mesh,
        in_specs=(both, rows, P(None, "tp"), P(None, "tp"), P("tp", None), both),
        out_specs=(both, both, P("dp", "tp"), P("dp", "tp"), P("tp", "dp")),
        check_vma=False,
    )
```

```python
import functools

import jax
import jax.numpy as jnp
from jax import lax
from jax.experimental import pallas as pl
from jax.experimental.pallas import tpu as pltpu
from jax.sharding import PartitionSpec as P

BF16 = jnp.bfloat16
F32 = jnp.float32
MESH = pl.DeviceIdType.MESH
D = 4096
W = 448
ROWS = 16
NZ = 8
HALF = 2048
CH = 512
TILE = 512
DEPTH = 2048


def kernel(
    tok, scale, cot, gw, uw, dw,
    mixed, tgrad, wout,
    nrm, ctg, ext, wg, wu, wd, acc, hid, gpr, glf, tra, got, part, crecv, zrecv, yst, yrecv,
    vch, vr1, vr2, vst, vrecv, wch, xr1, xr2, lsem, ssem, rsem,
):
    d, t = lax.axis_index("dp"), lax.axis_index("tp")
    yh, x = d // 4, d % 4
    z, yl, c = t // 4, (t // 2) % 2, t % 2
    zdev = {s: (d, ((z + s + NZ) % NZ) * 4 + yl * 2 + c) for s in (1, -1)}
    ydev = (d, z * 4 + (1 - yl) * 2 + c)
    cdev = (d, z * 4 + yl * 2 + (1 - c))
    xdev = {s: (yh * 4 + (x + s + 4) % 4, t) for s in (1, -1)}
    hdev = ((1 - yh) * 4 + x, t)
    partners = [zdev[1], zdev[-1], ydev, cdev, xdev[1], xdev[-1], hdev]

    barrier = pltpu.get_barrier_semaphore()
    for device in partners:
        pl.semaphore_signal(barrier, inc=1, device_id=device, device_id_type=MESH)

    loads = [
        pltpu.make_async_copy(src, dst, lsem.at[i])
        for i, (src, dst) in enumerate(((gw, wg), (uw, wu), (dw, wd)))
    ]
    for load in loads:
        load.start()

    sent = []

    def send(src, dst, device):
        at = len(sent)
        copy = pltpu.make_async_remote_copy(
            src_ref=src, dst_ref=dst, send_sem=ssem.at[at], recv_sem=rsem.at[at],
            device_id=device, device_id_type=MESH,
        )
        copy.start()
        sent.append(copy)
        return copy

    def normalized():
        xf = tok[...].astype(F32)
        r = lax.rsqrt(jnp.mean(xf * xf, axis=-1, keepdims=True) + 1e-05)
        return xf, r, xf * r

    nrm[z, yl, c] = (normalized()[2] * scale[...]).astype(BF16)
    ctg[z, yl, c] = cot[...]
    pl.semaphore_wait(barrier, len(partners))

    def gather(buf, width, base=0):
        def one(zz, y, s=0):
            mid = width // 2
            cols = {0: pl.ds(base, width), 1: pl.ds(base, mid), -1: pl.ds(base + mid, mid)}[s]
            return buf.at[zz, y, c, :, cols]

        def both(zz, s=0):
            mid = width // 2
            cols = {0: pl.ds(base, width), 1: pl.ds(base, mid), -1: pl.ds(base + mid, mid)}[s]
            return buf.at[zz, pl.ds(0, 2), c, :, cols]

        def push(ref, device):
            return send(ref, ref, device)

        at = {(s, h): (z - s * h + NZ) % NZ for s in (1, -1) for h in (1, 2, 3, 4)}
        ways = (1, -1)
        z1 = {s: push(one(z, yl), zdev[s]) for s in ways}
        y0 = push(one(z, yl), ydev)
        yield
        z2, y1 = {}, {}
        for s in ways:
            z1[s].wait_recv()
            z2[s] = push(one(at[s, 1], yl), zdev[s])
        yield
        y0.wait_recv()
        core = [push(both(z), cdev)]
        z3, y2, z3b = {}, {}, {}
        for s in ways:
            z2[s].wait_recv()
            z3[s] = push(one(at[s, 2], yl), zdev[s])
            y2[s] = push(one(at[s, 2], yl), ydev)
        yield
        for s in ways:
            y1[s] = push(one(at[s, 1], yl), ydev)
        for s in ways:
            y2[s].wait_recv()
            z3b[s] = push(one(at[s, 2], 1 - yl), zdev[s])
        yield
        z4, z4b = {}, {}
        for s in ways:
            core.append(push(both(at[s, 2]), cdev))
        for s in ways:
            z3[s].wait_recv()
            z4[s] = push(one(at[s, 3], yl, s), zdev[s])
        yield
        for s in ways:
            y1[s].wait_recv()
            core.append(push(both(at[s, 1]), cdev))
        for s in ways:
            z3b[s].wait_recv()
            z4b[s] = push(one(at[s, 3], 1 - yl, s), zdev[s])
            core.append(push(both(at[s, 3]), cdev))
        yield
        for s in ways:
            z4[s].wait_recv()
            z4b[s].wait_recv()
            core.append(push(both(at[s, 4], s), cdev))
        yield
        for copy in core:
            copy.wait_recv()

    def gather_pairs(buf, width, base=0):
        mid = width // 2

        def rows(zz, y, s=0):
            cols = {0: pl.ds(base, width), 1: pl.ds(base, mid), -1: pl.ds(base + mid, mid)}[s]
            return buf.at[zz, y, c, :, cols]

        def push(ref, device):
            return send(ref, ref, device)

        at = {(s, h): (z - s * h + NZ) % NZ for s in (1, -1) for h in (1, 2, 3, 4)}
        ways, core, own, other = (1, -1), [], {}, {}

        def on(zz, h, y, got):
            for s in ways:
                if h > 0:
                    got[s].wait_recv()
                place = zz if h == 0 else at[s, h]
                got[s] = push(rows(place, y, s if h == 3 else 0), zdev[s])

        def across(h, s, half=0):
            cols = {0: pl.ds(base, width), 1: pl.ds(base, mid), -1: pl.ds(base + mid, mid)}[half]
            ref = buf.at[z if h == 0 else at[s, h], pl.ds(0, 2), c, :, cols]
            core.append(push(ref, cdev))

        y0 = push(rows(z, yl), ydev)
        on(z, 0, yl, own)
        yield
        y0.wait_recv()
        on(z, 0, 1 - yl, other)
        across(0, 1)
        yield
        on(z, 1, yl, own)
        yield
        on(z, 1, 1 - yl, other)
        for s in ways:
            across(1, s)
        on(z, 2, yl, own)
        yield
        on(z, 2, 1 - yl, other)
        for s in ways:
            across(2, s)
        yield
        on(z, 3, yl, own)
        on(z, 3, 1 - yl, other)
        for s in ways:
            across(3, s)
        yield
        for s in ways:
            own[s].wait_recv()
            other[s].wait_recv()
            across(4, s, s)
        yield
        for copy in core:
            copy.wait_recv()

    def run(*gens):
        live = list(gens)
        while live:
            for g in list(live):
                if next(g, 1) == 1:
                    live.remove(g)

    half = pl.ds(pl.multiple_of((1 - yh) * HALF, HALF), HALF)
    most = 3584
    both_ways = [gather(buf, most) for buf in (nrm, ctg)]
    both_ways += [gather_pairs(buf, D - most, most) for buf in (nrm, ctg)]
    for way in both_ways:
        next(way)
    seed = send(nrm.at[z, yl, c, :, half], ext.at[z, yl, c], hdev)

    def seeded():
        seed.wait_recv()
        yield from gather_pairs(ext, HALF)

    third = seeded()
    run(*both_ways)
    next(third)

    def tokens_of(buf, col, width):
        return buf[:, :, :, :, pl.ds(col, width)].reshape(NZ * 4 * ROWS, width)

    acc[...] = jnp.zeros_like(acc)

    def into(i, buf, weight):
        @pl.loop(0, D // DEPTH)
        def _(k):
            at = pl.multiple_of(k * DEPTH, DEPTH)
            acc[i] += lax.dot_general(
                tokens_of(buf, at, DEPTH), weight[:, pl.ds(at, DEPTH)], (((1,), (1,)), ((), ())),
                preferred_element_type=F32,
            )

    for load in loads:
        load.wait()
    into(0, nrm, wg)
    next(third)
    into(1, nrm, wu)
    next(third)

    @pl.loop(0, 4)
    def _(k):
        rows = pl.ds(pl.multiple_of(k * 128, 128), 128)
        gate, lifted = acc[0, rows, :], acc[1, rows, :]
        h = gate * jax.nn.sigmoid(gate) * lifted
        hid[rows, :] = h.astype(BF16)
        tra[pl.ds(0, W), rows] = h.T.astype(BF16)

    next(third)

    def down(other, xx):
        at = pl.multiple_of(other * HALF + xx * CH, CH)
        return jnp.dot(tra[pl.ds(0, W), :], tokens_of(ctg, at, CH), preferred_element_type=F32)

    def downs():
        far = (x + 2) % 4
        after, before = (x + 1) % 4, (x + 3) % 4
        vch[0] = down(0, far).astype(BF16)
        one = send(vch.at[0], vr1.at[0], xdev[1])
        vch[1] = down(1, far).astype(BF16)
        two = send(vch.at[1], vr1.at[1], xdev[-1])
        vch[2] = down(1, after).astype(BF16)
        three = send(vch.at[2], vr2.at[0, 1], xdev[1])
        vch[3] = down(0, before).astype(BF16)
        four = send(vch.at[3], vr2.at[1, 0], xdev[-1])
        yield
        vch[4] = down(0, after).astype(BF16)
        vch[5] = down(1, before).astype(BF16)
        yield
        one.wait_recv()
        vch[4] = (vch[4].astype(F32) + vr1[0].astype(F32)).astype(BF16)
        five = send(vch.at[4], vr2.at[0, 0], xdev[1])
        two.wait_recv()
        vch[5] = (vch[5].astype(F32) + vr1[1].astype(F32)).astype(BF16)
        six = send(vch.at[5], vr2.at[1, 1], xdev[-1])
        yield
        theirs, mine = down(1 - yh, x), down(yh, x)
        for copy in (three, four, five, six):
            copy.wait_recv()
        vst[...] = (theirs + vr2[0, 1 - yh].astype(F32) + vr2[1, 1 - yh].astype(F32)).astype(BF16)
        last = send(vst, vrecv, hdev)
        yield
        mine = mine + vr2[0, yh].astype(F32) + vr2[1, yh].astype(F32)
        last.wait_recv()
        wout[pl.ds(0, W), :] = (mine + vrecv[...].astype(F32)).astype(BF16)

    down_sum = downs()
    next(down_sum)
    next(third)

    @pl.loop(0, D // TILE)
    def _(k):
        at = pl.multiple_of(k * TILE, TILE)
        out = jnp.dot(hid[...], wd[:, pl.ds(at, TILE)], preferred_element_type=F32)
        part[0, :, :, :, :, pl.ds(at, TILE)] = out.astype(BF16).reshape(NZ, 2, 2, ROWS, TILE)

    def s2(s):
        return 0 if s == 1 else 1

    def scatter(i):
        theirs = part.at[i, pl.ds(0, NZ), pl.ds(0, 2), 1 - c]
        core = send(theirs, crecv.at[i], cdev)
        yield
        core.wait_recv()
        arrived = {}
        for h in range(4):
            for s in (1, -1):
                zz = (z + s * (4 - h) + NZ) % NZ
                if h == 0:
                    cols = pl.ds(0, D // 2) if s == 1 else pl.ds(D // 2, D // 2)
                    total = part[i, zz, :, c, :, cols].astype(F32) + crecv[i, zz, :, :, cols].astype(F32)
                    part[i, zz, :, c, :, cols] = total.astype(BF16)
                else:
                    arrived[s].wait_recv()
                    for cols, added in (
                        (pl.ds(0, D // 2), h > 1 or s == 1),
                        (pl.ds(D // 2, D // 2), h > 1 or s == -1),
                    ):
                        total = part[i, zz, :, c, :, cols].astype(F32) + crecv[i, zz, :, :, cols].astype(F32)
                        if added:
                            total = total + zrecv[i, s2(s), h - 1, :, :, cols].astype(F32)
                        part[i, zz, :, c, :, cols] = total.astype(BF16)
                    cols = pl.ds(0, D)
                arrived[s] = send(
                    part.at[i, zz, pl.ds(0, 2), c, :, cols],
                    zrecv.at[i, s2(s), h, pl.ds(0, 2), :, cols],
                    zdev[s],
                )
            yield
        for s in (1, -1):
            arrived[s].wait_recv()

        def total_of(y):
            return (
                part[i, z, y, c].astype(F32) + crecv[i, z, y].astype(F32)
                + zrecv[i, 0, 3, y].astype(F32) + zrecv[i, 1, 3, y].astype(F32)
            )

        yst[i] = total_of(1 - yl).astype(BF16)
        last = send(yst.at[i], yrecv.at[i], ydev)
        yield
        last.wait_recv()
        total = total_of(yl) + yrecv[i].astype(F32)
        xf, r, unit = normalized()
        if i == 0:
            mixed[...] = (xf + total).astype(BF16)
        else:
            gain = total * scale[...]
            inner = jnp.mean(gain * unit, axis=-1, keepdims=True)
            tgrad[...] = (cot[...].astype(F32) + r * (gain - unit * inner)).astype(BF16)

    forward = scatter(0)
    next(forward)
    next(third)
    into(2, ctg, wd)
    next(forward)
    next(third)

    @pl.loop(0, 4)
    def _(k):
        rows = pl.ds(pl.multiple_of(k * 128, 128), 128)
        gate, lifted, gh = acc[0, rows, :], acc[1, rows, :], acc[2, rows, :]
        sg = jax.nn.sigmoid(gate)
        gp = gh * lifted * sg * (1.0 + gate * (1.0 - sg))
        gl = gh * (gate * sg)
        gpr[rows, :] = gp.astype(BF16)
        glf[rows, :] = gl.astype(BF16)
        tra[pl.ds(W, W), rows] = gp.T.astype(BF16)
        tra[pl.ds(2 * W, W), rows] = gl.T.astype(BF16)

    swaps = []
    for g in range(2):
        rows = pl.ds((g + 1) * W, W)
        swaps.append(send(tra.at[rows], got.at[g], hdev))

    next(down_sum)

    @pl.loop(0, D // TILE)
    def _(k):
        at = pl.multiple_of(k * TILE, TILE)
        out = jnp.dot(gpr[...], wg[:, pl.ds(at, TILE)], preferred_element_type=F32)
        out += jnp.dot(glf[...], wu[:, pl.ds(at, TILE)], preferred_element_type=F32)
        part[1, :, :, :, :, pl.ds(at, TILE)] = out.astype(BF16).reshape(NZ, 2, 2, ROWS, TILE)

    backward = scatter(1)
    next(backward)
    run(third)
    next(forward)
    next(down_sum)
    next(backward)

    q = W // 2

    def weights(g, xx):
        at = pl.multiple_of(yh * HALF + xx * CH, CH)
        far = pl.multiple_of(xx * CH, CH)
        out = jnp.dot(tra[pl.ds((g + 1) * W, W), :], tokens_of(nrm, at, CH), preferred_element_type=F32)
        out += jnp.dot(got[g], tokens_of(ext, far, CH), preferred_element_type=F32)
        return out

    def over_x(g):
        up, down = pl.ds(0, q), pl.ds(q, q)
        swaps[g].wait_recv()
        far = (x + 2) % 4
        wch[g, 0] = weights(g, far).astype(BF16)
        one = send(wch.at[g, 0, up], xr1.at[g, 0], xdev[1])
        two = send(wch.at[g, 0, down], xr1.at[g, 1], xdev[-1])
        wch[g, 1] = weights(g, (x + 1) % 4).astype(BF16)
        three = send(wch.at[g, 1, down], xr2.at[g, 0, down], xdev[1])
        wch[g, 2] = weights(g, (x + 3) % 4).astype(BF16)
        four = send(wch.at[g, 2, up], xr2.at[g, 1, up], xdev[-1])
        yield
        one.wait_recv()
        wch[g, 1, up] = (wch[g, 1, up].astype(F32) + xr1[g, 0].astype(F32)).astype(BF16)
        five = send(wch.at[g, 1, up], xr2.at[g, 0, up], xdev[1])
        two.wait_recv()
        wch[g, 2, down] = (wch[g, 2, down].astype(F32) + xr1[g, 1].astype(F32)).astype(BF16)
        six = send(wch.at[g, 2, down], xr2.at[g, 1, down], xdev[-1])
        yield
        mine = weights(g, x)
        for copy in (three, four, five, six):
            copy.wait_recv()
        total = mine + xr2[g, 0].astype(F32) + xr2[g, 1].astype(F32)
        wout[pl.ds((g + 1) * W, W), :] = total.astype(BF16)

    gate_sum, up_sum = over_x(0), over_x(1)
    next(forward)
    next(backward)
    next(gate_sum)
    next(forward)
    next(backward)
    next(up_sum)
    next(down_sum)
    next(forward)
    next(backward)
    next(gate_sum)
    run(forward)
    next(backward)
    run(down_sum)
    next(up_sum)
    run(backward)
    run(gate_sum)
    run(up_sum)

    for copy in sent:
        copy.wait_send()


def finish(mixed, tgrad, wout, mixed_out, tgrad_out, gate_out, up_out, down_out):
    mixed_out[...] = mixed[...]
    tgrad_out[...] = tgrad[...]
    gate_out[...] = wout[W : 2 * W]
    up_out[...] = wout[2 * W :]
    down_out[...] = wout[:W]


def local(tokens, norm_scale_vector, gate_weight, up_weight, down_weight, cotangent):
    vmem = pl.BlockSpec(memory_space=pltpu.VMEM)
    hbm = pl.BlockSpec(memory_space=pl.ANY)
    slab = (NZ, 2, 2, ROWS, D)
    count = 216
    mixed, tgrad, wout = pl.pallas_call(
        kernel,
        out_shape=(
            jax.ShapeDtypeStruct((ROWS, D), BF16),
            jax.ShapeDtypeStruct((ROWS, D), BF16),
            jax.ShapeDtypeStruct((3 * W, CH), BF16),
        ),
        in_specs=[vmem, vmem, vmem, hbm, hbm, hbm],
        out_specs=(vmem, vmem, vmem),
        scratch_shapes=[
            pltpu.VMEM(slab, BF16),
            pltpu.VMEM(slab, BF16),
            pltpu.VMEM((NZ, 2, 2, ROWS, HALF), BF16),
            pltpu.VMEM((W, D), BF16),
            pltpu.VMEM((W, D), BF16),
            pltpu.VMEM((W, D), BF16),
            pltpu.VMEM((3, 512, W), F32),
            pltpu.VMEM((512, W), BF16),
            pltpu.VMEM((512, W), BF16),
            pltpu.VMEM((512, W), BF16),
            pltpu.VMEM((3 * W, 512), BF16),
            pltpu.VMEM((2, W, 512), BF16),
            pltpu.VMEM((2, *slab), BF16),
            pltpu.VMEM((2, NZ, 2, ROWS, D), BF16),
            pltpu.VMEM((2, 2, 4, 2, ROWS, D), BF16),
            pltpu.VMEM((2, ROWS, D), BF16),
            pltpu.VMEM((2, ROWS, D), BF16),
            pltpu.VMEM((6, W, CH), BF16),
            pltpu.VMEM((2, W, CH), BF16),
            pltpu.VMEM((2, 2, W, CH), BF16),
            pltpu.VMEM((W, CH), BF16),
            pltpu.VMEM((W, CH), BF16),
            pltpu.VMEM((2, 3, W, CH), BF16),
            pltpu.VMEM((2, 2, W // 2, CH), BF16),
            pltpu.VMEM((2, 2, W, CH), BF16),
            pltpu.SemaphoreType.DMA((3,)),
            pltpu.SemaphoreType.DMA((count,)),
            pltpu.SemaphoreType.DMA((count,)),
        ],
        compiler_params=pltpu.CompilerParams(
            collective_id=0, has_side_effects=True, vmem_limit_bytes=62 << 20
        ),
        cost_estimate=pl.CostEstimate(
            flops=2 * 9 * 512 * D * W, bytes_accessed=16 << 20, transcendentals=512 * W
        ),
        name="ffn",
    )(tokens, norm_scale_vector.reshape(1, D), cotangent, gate_weight.T, up_weight.T, down_weight)
    block = jax.ShapeDtypeStruct((W, CH), BF16)
    mixed, tgrad, gate, up, down = pl.pallas_call(
        finish,
        out_shape=(*(jax.ShapeDtypeStruct(v.shape, v.dtype) for v in (mixed, tgrad)), block, block, block),
        in_specs=[vmem] * 3,
        out_specs=(vmem,) * 5,
        compiler_params=pltpu.CompilerParams(vmem_limit_bytes=62 << 20),
        name="finish",
    )(mixed, tgrad, wout)
    return mixed, tgrad, gate.T, up.T, down


def solution(mesh):
    both, rows = P(("dp", "tp"), None), P()
    return jax.shard_map(
        local,
        mesh=mesh,
        in_specs=(both, rows, P(None, "tp"), P(None, "tp"), P("tp", None), both),
        out_specs=(both, both, P("dp", "tp"), P("dp", "tp"), P("tp", "dp")),
        check_vma=False,
    )
```

```python
import functools

import jax
import jax.numpy as jnp
from jax import lax
from jax.experimental import pallas as pl
from jax.experimental.pallas import tpu as pltpu
from jax.sharding import PartitionSpec as P

BF16 = jnp.bfloat16
F32 = jnp.float32
MESH = pl.DeviceIdType.MESH
D = 4096
W = 448
ROWS = 16
NZ = 8
HALF = 2048
CH = 512
TILE = 512
DEPTH = 2048


def kernel(
    tok, scale, cot, gw, uw, dw,
    mixed, tgrad, wout,
    nrm, ctg, ext, wg, wu, wd, acc, hid, gpr, glf, tra, got, part, crecv, zrecv, yst, yrecv,
    vch, vr1, vr2, vst, vrecv, wch, xr1, xr2, lsem, ssem, rsem,
):
    d, t = lax.axis_index("dp"), lax.axis_index("tp")
    yh, x = d // 4, d % 4
    z, yl, c = t // 4, (t // 2) % 2, t % 2
    zdev = {s: (d, ((z + s + NZ) % NZ) * 4 + yl * 2 + c) for s in (1, -1)}
    ydev = (d, z * 4 + (1 - yl) * 2 + c)
    cdev = (d, z * 4 + yl * 2 + (1 - c))
    xdev = {s: (yh * 4 + (x + s + 4) % 4, t) for s in (1, -1)}
    hdev = ((1 - yh) * 4 + x, t)
    partners = [zdev[1], zdev[-1], ydev, cdev, xdev[1], xdev[-1], hdev]

    barrier = pltpu.get_barrier_semaphore()
    for device in partners:
        pl.semaphore_signal(barrier, inc=1, device_id=device, device_id_type=MESH)

    loads = [
        pltpu.make_async_copy(src, dst, lsem.at[i])
        for i, (src, dst) in enumerate(((gw, wg), (uw, wu), (dw, wd)))
    ]
    for load in loads:
        load.start()

    sent = []

    def send(src, dst, device):
        at = len(sent)
        copy = pltpu.make_async_remote_copy(
            src_ref=src, dst_ref=dst, send_sem=ssem.at[at], recv_sem=rsem.at[at],
            device_id=device, device_id_type=MESH,
        )
        copy.start()
        sent.append(copy)
        return copy

    def normalized():
        xf = tok[...].astype(F32)
        r = lax.rsqrt(jnp.mean(xf * xf, axis=-1, keepdims=True) + 1e-05)
        return xf, r, xf * r

    nrm[z, yl, c] = (normalized()[2] * scale[...]).astype(BF16)
    ctg[z, yl, c] = cot[...]
    pl.semaphore_wait(barrier, len(partners))

    def gather(buf, width, base=0):
        def one(zz, y, s=0):
            mid = width // 2
            cols = {0: pl.ds(base, width), 1: pl.ds(base, mid), -1: pl.ds(base + mid, mid)}[s]
            return buf.at[zz, y, c, :, cols]

        def both(zz, s=0):
            mid = width // 2
            cols = {0: pl.ds(base, width), 1: pl.ds(base, mid), -1: pl.ds(base + mid, mid)}[s]
            return buf.at[zz, pl.ds(0, 2), c, :, cols]

        def push(ref, device):
            return send(ref, ref, device)

        at = {(s, h): (z - s * h + NZ) % NZ for s in (1, -1) for h in (1, 2, 3, 4)}
        ways = (1, -1)
        z1 = {s: push(one(z, yl), zdev[s]) for s in ways}
        y0 = push(one(z, yl), ydev)
        yield
        z2, y1 = {}, {}
        for s in ways:
            z1[s].wait_recv()
            z2[s] = push(one(at[s, 1], yl), zdev[s])
        yield
        y0.wait_recv()
        core = [push(both(z), cdev)]
        z3, y2, z3b = {}, {}, {}
        for s in ways:
            z2[s].wait_recv()
            z3[s] = push(one(at[s, 2], yl), zdev[s])
            y2[s] = push(one(at[s, 2], yl), ydev)
        yield
        for s in ways:
            y1[s] = push(one(at[s, 1], yl), ydev)
        for s in ways:
            y2[s].wait_recv()
            z3b[s] = push(one(at[s, 2], 1 - yl), zdev[s])
        yield
        z4, z4b = {}, {}
        for s in ways:
            core.append(push(both(at[s, 2]), cdev))
        for s in ways:
            z3[s].wait_recv()
            z4[s] = push(one(at[s, 3], yl, s), zdev[s])
        yield
        for s in ways:
            y1[s].wait_recv()
            core.append(push(both(at[s, 1]), cdev))
        for s in ways:
            z3b[s].wait_recv()
            z4b[s] = push(one(at[s, 3], 1 - yl, s), zdev[s])
            core.append(push(both(at[s, 3]), cdev))
        yield
        for s in ways:
            z4[s].wait_recv()
            z4b[s].wait_recv()
            core.append(push(both(at[s, 4], s), cdev))
        yield
        for copy in core:
            copy.wait_recv()

    def gather_pairs(buf, width, base=0):
        mid = width // 2

        def rows(zz, y, s=0):
            cols = {0: pl.ds(base, width), 1: pl.ds(base, mid), -1: pl.ds(base + mid, mid)}[s]
            return buf.at[zz, y, c, :, cols]

        def push(ref, device):
            return send(ref, ref, device)

        at = {(s, h): (z - s * h + NZ) % NZ for s in (1, -1) for h in (1, 2, 3, 4)}
        ways, core, own, other = (1, -1), [], {}, {}

        def on(zz, h, y, got):
            for s in ways:
                if h > 0:
                    got[s].wait_recv()
                place = zz if h == 0 else at[s, h]
                got[s] = push(rows(place, y, s if h == 3 else 0), zdev[s])

        def across(h, s, half=0):
            cols = {0: pl.ds(base, width), 1: pl.ds(base, mid), -1: pl.ds(base + mid, mid)}[half]
            ref = buf.at[z if h == 0 else at[s, h], pl.ds(0, 2), c, :, cols]
            core.append(push(ref, cdev))

        y0 = push(rows(z, yl), ydev)
        on(z, 0, yl, own)
        yield
        y0.wait_recv()
        on(z, 0, 1 - yl, other)
        across(0, 1)
        yield
        on(z, 1, yl, own)
        yield
        on(z, 1, 1 - yl, other)
        for s in ways:
            across(1, s)
        on(z, 2, yl, own)
        yield
        on(z, 2, 1 - yl, other)
        for s in ways:
            across(2, s)
        yield
        on(z, 3, yl, own)
        on(z, 3, 1 - yl, other)
        for s in ways:
            across(3, s)
        yield
        for s in ways:
            own[s].wait_recv()
            other[s].wait_recv()
            across(4, s, s)
        yield
        for copy in core:
            copy.wait_recv()

    def run(*gens):
        live = list(gens)
        while live:
            for g in list(live):
                if next(g, 1) == 1:
                    live.remove(g)

    half = pl.ds(pl.multiple_of((1 - yh) * HALF, HALF), HALF)
    most = 3584
    both_ways = [gather(buf, most) for buf in (nrm, ctg)]
    both_ways += [gather_pairs(buf, D - most, most) for buf in (nrm, ctg)]
    for way in both_ways:
        next(way)
    seed = send(nrm.at[z, yl, c, :, half], ext.at[z, yl, c], hdev)

    def seeded():
        seed.wait_recv()
        yield from gather_pairs(ext, HALF)

    third = seeded()
    run(*both_ways)
    next(third)

    def tokens_of(buf, col, width):
        return buf[:, :, :, :, pl.ds(col, width)].reshape(NZ * 4 * ROWS, width)

    def into(i, buf, weight):
        dims = (((1,), (1,)), ((), ()))
        first, second = (
            lax.dot_general(
                tokens_of(buf, at, DEPTH), weight[:, pl.ds(at, DEPTH)], dims,
                preferred_element_type=F32,
            )
            for at in (0, DEPTH)
        )
        acc[i] = first + second

    for load in loads:
        load.wait()
    into(0, nrm, wg)
    next(third)
    into(1, nrm, wu)
    next(third)

    @pl.loop(0, 4)
    def _(k):
        rows = pl.ds(pl.multiple_of(k * 128, 128), 128)
        gate, lifted = acc[0, rows, :], acc[1, rows, :]
        h = gate * jax.nn.sigmoid(gate) * lifted
        hid[rows, :] = h.astype(BF16)
        tra[pl.ds(0, W), rows] = h.T.astype(BF16)

    next(third)

    def down(other, xx):
        at = pl.multiple_of(other * HALF + xx * CH, CH)
        return jnp.dot(tra[pl.ds(0, W), :], tokens_of(ctg, at, CH), preferred_element_type=F32)

    def downs():
        far = (x + 2) % 4
        after, before = (x + 1) % 4, (x + 3) % 4
        vch[0] = down(0, far).astype(BF16)
        one = send(vch.at[0], vr1.at[0], xdev[1])
        vch[1] = down(1, far).astype(BF16)
        two = send(vch.at[1], vr1.at[1], xdev[-1])
        vch[2] = down(1, after).astype(BF16)
        three = send(vch.at[2], vr2.at[0, 1], xdev[1])
        vch[3] = down(0, before).astype(BF16)
        four = send(vch.at[3], vr2.at[1, 0], xdev[-1])
        yield
        vch[4] = down(0, after).astype(BF16)
        vch[5] = down(1, before).astype(BF16)
        yield
        one.wait_recv()
        vch[4] = (vch[4].astype(F32) + vr1[0].astype(F32)).astype(BF16)
        five = send(vch.at[4], vr2.at[0, 0], xdev[1])
        two.wait_recv()
        vch[5] = (vch[5].astype(F32) + vr1[1].astype(F32)).astype(BF16)
        six = send(vch.at[5], vr2.at[1, 1], xdev[-1])
        yield
        theirs, mine = down(1 - yh, x), down(yh, x)
        for copy in (three, four, five, six):
            copy.wait_recv()
        vst[...] = (theirs + vr2[0, 1 - yh].astype(F32) + vr2[1, 1 - yh].astype(F32)).astype(BF16)
        last = send(vst, vrecv, hdev)
        yield
        mine = mine + vr2[0, yh].astype(F32) + vr2[1, yh].astype(F32)
        last.wait_recv()
        wout[pl.ds(0, W), :] = (mine + vrecv[...].astype(F32)).astype(BF16)

    down_sum = downs()
    next(down_sum)
    next(third)

    @pl.loop(0, D // TILE)
    def _(k):
        at = pl.multiple_of(k * TILE, TILE)
        out = jnp.dot(hid[...], wd[:, pl.ds(at, TILE)], preferred_element_type=F32)
        part[0, :, :, :, :, pl.ds(at, TILE)] = out.astype(BF16).reshape(NZ, 2, 2, ROWS, TILE)

    def s2(s):
        return 0 if s == 1 else 1

    def scatter(i):
        theirs = part.at[i, pl.ds(0, NZ), pl.ds(0, 2), 1 - c]
        core = send(theirs, crecv.at[i], cdev)
        yield
        core.wait_recv()
        arrived = {}
        for h in range(4):
            for s in (1, -1):
                zz = (z + s * (4 - h) + NZ) % NZ
                if h == 0:
                    cols = pl.ds(0, D // 2) if s == 1 else pl.ds(D // 2, D // 2)
                    total = part[i, zz, :, c, :, cols].astype(F32) + crecv[i, zz, :, :, cols].astype(F32)
                    part[i, zz, :, c, :, cols] = total.astype(BF16)
                else:
                    arrived[s].wait_recv()
                    for cols, added in (
                        (pl.ds(0, D // 2), h > 1 or s == 1),
                        (pl.ds(D // 2, D // 2), h > 1 or s == -1),
                    ):
                        total = part[i, zz, :, c, :, cols].astype(F32) + crecv[i, zz, :, :, cols].astype(F32)
                        if added:
                            total = total + zrecv[i, s2(s), h - 1, :, :, cols].astype(F32)
                        part[i, zz, :, c, :, cols] = total.astype(BF16)
                    cols = pl.ds(0, D)
                arrived[s] = send(
                    part.at[i, zz, pl.ds(0, 2), c, :, cols],
                    zrecv.at[i, s2(s), h, pl.ds(0, 2), :, cols],
                    zdev[s],
                )
            yield
        for s in (1, -1):
            arrived[s].wait_recv()

        def total_of(y):
            return (
                part[i, z, y, c].astype(F32) + crecv[i, z, y].astype(F32)
                + zrecv[i, 0, 3, y].astype(F32) + zrecv[i, 1, 3, y].astype(F32)
            )

        yst[i] = total_of(1 - yl).astype(BF16)
        last = send(yst.at[i], yrecv.at[i], ydev)
        yield
        last.wait_recv()
        total = total_of(yl) + yrecv[i].astype(F32)
        xf, r, unit = normalized()
        if i == 0:
            mixed[...] = (xf + total).astype(BF16)
        else:
            gain = total * scale[...]
            inner = jnp.mean(gain * unit, axis=-1, keepdims=True)
            tgrad[...] = (cot[...].astype(F32) + r * (gain - unit * inner)).astype(BF16)

    forward = scatter(0)
    next(forward)
    next(third)
    into(2, ctg, wd)
    next(forward)
    next(third)

    @pl.loop(0, 4)
    def _(k):
        rows = pl.ds(pl.multiple_of(k * 128, 128), 128)
        gate, lifted, gh = acc[0, rows, :], acc[1, rows, :], acc[2, rows, :]
        sg = jax.nn.sigmoid(gate)
        gp = gh * lifted * sg * (1.0 + gate * (1.0 - sg))
        gl = gh * (gate * sg)
        gpr[rows, :] = gp.astype(BF16)
        glf[rows, :] = gl.astype(BF16)
        tra[pl.ds(W, W), rows] = gp.T.astype(BF16)
        tra[pl.ds(2 * W, W), rows] = gl.T.astype(BF16)

    swaps = []
    for g in range(2):
        rows = pl.ds((g + 1) * W, W)
        swaps.append(send(tra.at[rows], got.at[g], hdev))

    next(down_sum)

    @pl.loop(0, D // TILE)
    def _(k):
        at = pl.multiple_of(k * TILE, TILE)
        out = jnp.dot(gpr[...], wg[:, pl.ds(at, TILE)], preferred_element_type=F32)
        out += jnp.dot(glf[...], wu[:, pl.ds(at, TILE)], preferred_element_type=F32)
        part[1, :, :, :, :, pl.ds(at, TILE)] = out.astype(BF16).reshape(NZ, 2, 2, ROWS, TILE)

    backward = scatter(1)
    next(backward)
    run(third)
    next(forward)
    next(down_sum)
    next(backward)

    q = W // 2

    def weights(g, xx):
        at = pl.multiple_of(yh * HALF + xx * CH, CH)
        far = pl.multiple_of(xx * CH, CH)
        out = jnp.dot(tra[pl.ds((g + 1) * W, W), :], tokens_of(nrm, at, CH), preferred_element_type=F32)
        out += jnp.dot(got[g], tokens_of(ext, far, CH), preferred_element_type=F32)
        return out

    def over_x(g):
        up, down = pl.ds(0, q), pl.ds(q, q)
        swaps[g].wait_recv()
        far = (x + 2) % 4
        wch[g, 0] = weights(g, far).astype(BF16)
        one = send(wch.at[g, 0, up], xr1.at[g, 0], xdev[1])
        two = send(wch.at[g, 0, down], xr1.at[g, 1], xdev[-1])
        wch[g, 1] = weights(g, (x + 1) % 4).astype(BF16)
        three = send(wch.at[g, 1, down], xr2.at[g, 0, down], xdev[1])
        wch[g, 2] = weights(g, (x + 3) % 4).astype(BF16)
        four = send(wch.at[g, 2, up], xr2.at[g, 1, up], xdev[-1])
        yield
        one.wait_recv()
        wch[g, 1, up] = (wch[g, 1, up].astype(F32) + xr1[g, 0].astype(F32)).astype(BF16)
        five = send(wch.at[g, 1, up], xr2.at[g, 0, up], xdev[1])
        two.wait_recv()
        wch[g, 2, down] = (wch[g, 2, down].astype(F32) + xr1[g, 1].astype(F32)).astype(BF16)
        six = send(wch.at[g, 2, down], xr2.at[g, 1, down], xdev[-1])
        yield
        mine = weights(g, x)
        for copy in (three, four, five, six):
            copy.wait_recv()
        total = mine + xr2[g, 0].astype(F32) + xr2[g, 1].astype(F32)
        wout[pl.ds((g + 1) * W, W), :] = total.astype(BF16)

    gate_sum, up_sum = over_x(0), over_x(1)
    next(forward)
    next(backward)
    next(gate_sum)
    next(forward)
    next(backward)
    next(up_sum)
    next(down_sum)
    next(forward)
    next(backward)
    next(gate_sum)
    run(forward)
    next(backward)
    run(down_sum)
    next(up_sum)
    run(backward)
    run(gate_sum)
    run(up_sum)

    for copy in sent:
        copy.wait_send()


def finish(mixed, tgrad, wout, mixed_out, tgrad_out, gate_out, up_out, down_out):
    mixed_out[...] = mixed[...]
    tgrad_out[...] = tgrad[...]
    gate_out[...] = wout[W : 2 * W]
    up_out[...] = wout[2 * W :]
    down_out[...] = wout[:W]


def local(tokens, norm_scale_vector, gate_weight, up_weight, down_weight, cotangent):
    vmem = pl.BlockSpec(memory_space=pltpu.VMEM)
    hbm = pl.BlockSpec(memory_space=pl.ANY)
    slab = (NZ, 2, 2, ROWS, D)
    count = 216
    mixed, tgrad, wout = pl.pallas_call(
        kernel,
        out_shape=(
            jax.ShapeDtypeStruct((ROWS, D), BF16),
            jax.ShapeDtypeStruct((ROWS, D), BF16),
            jax.ShapeDtypeStruct((3 * W, CH), BF16),
        ),
        in_specs=[vmem, vmem, vmem, hbm, hbm, hbm],
        out_specs=(vmem, vmem, vmem),
        scratch_shapes=[
            pltpu.VMEM(slab, BF16),
            pltpu.VMEM(slab, BF16),
            pltpu.VMEM((NZ, 2, 2, ROWS, HALF), BF16),
            pltpu.VMEM((W, D), BF16),
            pltpu.VMEM((W, D), BF16),
            pltpu.VMEM((W, D), BF16),
            pltpu.VMEM((3, 512, W), F32),
            pltpu.VMEM((512, W), BF16),
            pltpu.VMEM((512, W), BF16),
            pltpu.VMEM((512, W), BF16),
            pltpu.VMEM((3 * W, 512), BF16),
            pltpu.VMEM((2, W, 512), BF16),
            pltpu.VMEM((2, *slab), BF16),
            pltpu.VMEM((2, NZ, 2, ROWS, D), BF16),
            pltpu.VMEM((2, 2, 4, 2, ROWS, D), BF16),
            pltpu.VMEM((2, ROWS, D), BF16),
            pltpu.VMEM((2, ROWS, D), BF16),
            pltpu.VMEM((6, W, CH), BF16),
            pltpu.VMEM((2, W, CH), BF16),
            pltpu.VMEM((2, 2, W, CH), BF16),
            pltpu.VMEM((W, CH), BF16),
            pltpu.VMEM((W, CH), BF16),
            pltpu.VMEM((2, 3, W, CH), BF16),
            pltpu.VMEM((2, 2, W // 2, CH), BF16),
            pltpu.VMEM((2, 2, W, CH), BF16),
            pltpu.SemaphoreType.DMA((3,)),
            pltpu.SemaphoreType.DMA((count,)),
            pltpu.SemaphoreType.DMA((count,)),
        ],
        compiler_params=pltpu.CompilerParams(
            collective_id=0, has_side_effects=True, vmem_limit_bytes=62 << 20
        ),
        cost_estimate=pl.CostEstimate(
            flops=2 * 9 * 512 * D * W, bytes_accessed=16 << 20, transcendentals=512 * W
        ),
        name="ffn",
    )(tokens, norm_scale_vector.reshape(1, D), cotangent, gate_weight.T, up_weight.T, down_weight)
    block = jax.ShapeDtypeStruct((W, CH), BF16)
    mixed, tgrad, gate, up, down = pl.pallas_call(
        finish,
        out_shape=(*(jax.ShapeDtypeStruct(v.shape, v.dtype) for v in (mixed, tgrad)), block, block, block),
        in_specs=[vmem] * 3,
        out_specs=(vmem,) * 5,
        compiler_params=pltpu.CompilerParams(vmem_limit_bytes=62 << 20),
        name="finish",
    )(mixed, tgrad, wout)
    return mixed, tgrad, gate.T, up.T, down


def solution(mesh):
    both, rows = P(("dp", "tp"), None), P()
    return jax.shard_map(
        local,
        mesh=mesh,
        in_specs=(both, rows, P(None, "tp"), P(None, "tp"), P("tp", None), both),
        out_specs=(both, both, P("dp", "tp"), P("dp", "tp"), P("tp", "dp")),
        check_vma=False,
    )
```
